32 devices in a mesh: kv: 2 (over y), key: 4 (over z), tok: 4 (over x, core).
Axes of the slice: x: 2, y: 2, z: 4, core: 2. Of those that a mesh axis runs over, the one named last changes fastest.
Arguments:
- queries: bfloat16 [1024, 8192], P('key', ('kv', 'tok')), may hold values from -200 to 200
- keys: bfloat16 [1024, 1024], P('key', 'kv'), may hold values from -8 to 8
- values: bfloat16 [1024, 1024], P('key', 'kv'), may hold values from -6 to 6
- doc_ids: int32 [1024], replicated, may hold values from 0 to 5, never falling along the last dimension, each value on 1 to 512 neighbouring positions
- out_weight: bfloat16 [8192, 8192], P('kv', 'tok'), may hold values from -0.0625 to 0.0625
Outputs:
- mixed: bfloat16 [1024, 8192], P(('key', 'kv'), 'tok')
The draws below stay inside these ranges and needn't reach their ends.
Inputs may be any that keep to these rules, and one draw needn't show every extreme that they name: `doc_ids`: document numbers never fall along the window; a document covers at most 512 positions and some document covers exactly that many.
All inputs are finite; a program needn't handle non-finite values.
Results may differ from the reference program's by a relative error of at most 0.014.
Values may be sent and summed in bfloat16 or wider, within the bound.
A program may use at most 64 MiB of HBM per device.

```python
import math
import jax
import jax.numpy as jnp
import numpy as np
from jax import lax

D = 8192
QUERY_HEADS = 64
KEY_VALUE_HEADS = 8
HEAD_SIZE = 128
TOK_DEV = 256
REACH = 2
WINDOW_TOKENS = 1024
N_KEY = 4


def closing_keys(key):
    sampled_rows = jnp.clip(jax.random.normal(jax.random.fold_in(key, 11), (WINDOW_TOKENS, KEY_VALUE_HEADS * HEAD_SIZE), jnp.float32), -6.0, 6.0)
    return sampled_rows


def draw_keys(key, part):
    return closing_keys(key).astype(jnp.bfloat16)


def draw_queries(key, part):
    sampled_rows = 2.5 * jnp.clip(jax.random.normal(jax.random.fold_in(key, 21), (WINDOW_TOKENS, QUERY_HEADS * HEAD_SIZE), jnp.float32), -6.0, 6.0)
    return sampled_rows.astype(jnp.bfloat16)


def block_levels(rng, dims, cuts, low, high):
    level, own = 1.0, jax.random.fold_in(rng, 6)
    for dim, blocks in cuts:
        steps = jnp.exp(jax.random.uniform(jax.random.fold_in(own, dim), (blocks,), jnp.float32, low / len(cuts), high / len(cuts)))
        level = level * jnp.repeat(steps, dims[dim] // blocks).reshape([-1 if axis == dim else 1 for axis in range(len(dims))])
    return level


def length_profile(count, total, bound, lean):
    loads = [(1 << 20) // math.isqrt(standing ** lean) + 1 for standing in range(2, count + 1)]
    surplus, holding = total - bound - (count - 1), [1] * (count - 1)
    while surplus > 0:
        movable = [i for i in range(count - 1) if holding[i] < bound]
        pool, budget = sum([loads[i] for i in movable]), surplus
        for i in movable:
            addition = min(bound - holding[i], max(1, budget * loads[i] // pool), surplus)
            holding[i] = holding[i] + addition
            surplus = surplus - addition
    return np.array([bound] + holding)


def uneven_parts(key, count, total, bound, slope):
    if count == 2:
        one = jax.random.randint(key, (), max(1, total - bound), min(bound, total - 1) + 1)
        return jnp.stack([one, total - one])
    sizes = jnp.asarray(length_profile(count, total, bound, slope), jnp.int32)
    pairs = (count - 1) // 2
    giver, receiver = sizes[1:1 + 2 * pairs:2], sizes[2:2 + 2 * pairs:2]
    room = jnp.minimum(giver - 1, bound - receiver)
    shifted = jax.random.randint(jax.random.fold_in(key, 1), (pairs,), 0, 1 << 20) % (room + 1)
    sizes = sizes.at[1:1 + 2 * pairs:2].set(giver - shifted).at[2:2 + 2 * pairs:2].set(receiver + shifted)
    return sizes[jax.random.permutation(jax.random.fold_in(key, 2), count)]


def noise(key, dims, spread, reach, split=(), kind=jnp.bfloat16):
    level = block_levels(key, dims, split, -0.22, 0.18) if split else 1.0
    result = jax.random.normal(key, dims, jnp.float32) * spread * level
    return jnp.minimum(jnp.maximum(result, -reach), reach).astype(kind)


def setup_inputs(seed: int = 0) -> dict:
    arg_keys = jax.random.split(jax.random.key(seed), 6)
    queries = draw_queries(jax.random.fold_in(arg_keys[5], 71), 0)
    keys = draw_keys(jax.random.fold_in(arg_keys[5], 71), 0)
    values = noise(arg_keys[2], (WINDOW_TOKENS, KEY_VALUE_HEADS * HEAD_SIZE), 1.0, 6.0, ((0, 4), (1, 2)))
    doc_ids = jnp.searchsorted(jnp.cumsum(uneven_parts(arg_keys[3], 6, WINDOW_TOKENS, REACH * TOK_DEV, 2)), jnp.arange(WINDOW_TOKENS), side="right").astype(jnp.int32)
    out_weight = noise(arg_keys[4], (QUERY_HEADS * HEAD_SIZE, D), (QUERY_HEADS * HEAD_SIZE) ** -0.5, 0.0625, ((0, 2), (1, 4)))
    return {"queries": queries, "keys": keys, "values": values, "doc_ids": doc_ids, "out_weight": out_weight}


very_low = -1e+30

def partial_block(query_block, key_block, value_block, query_docs, key_docs, query_pos, key_pos):
    group_width = QUERY_HEADS // KEY_VALUE_HEADS
    key_wide = jnp.repeat(key_block, group_width, axis=1).astype(jnp.float32)
    value_wide = jnp.repeat(value_block, group_width, axis=1).astype(jnp.float32)
    scores = jnp.einsum('qhd,shd->hqs', query_block.astype(jnp.float32), key_wide) * (1.0 / math.sqrt(HEAD_SIZE))
    allowed = (query_docs[:, None] == key_docs[None, :]) & (key_pos[None, :] <= query_pos[:, None])
    highest = lax.optimization_barrier(jnp.max(jnp.where(allowed[None], scores, very_low), axis=2))
    weights = jnp.exp(jnp.where(allowed[None], scores - highest[:, :, None], very_low))
    totals = lax.optimization_barrier(jnp.sum(weights, axis=2)).T
    probs = weights.astype(jnp.bfloat16)
    weighted = jnp.einsum('hqs,shd->qhd', probs.astype(jnp.float32), value_wide)
    positive = totals > 0
    safe = jnp.where(positive, totals, 1.0)
    piece = (weighted / safe[:, :, None]).astype(jnp.bfloat16)
    log_total = jnp.where(positive, highest.T + jnp.log(safe), very_low)
    return (piece, log_total)

def reference(queries, keys, values, doc_ids, out_weight):
    query_three = queries.reshape(WINDOW_TOKENS, QUERY_HEADS, HEAD_SIZE)
    key_cube = keys.reshape(WINDOW_TOKENS, KEY_VALUE_HEADS, HEAD_SIZE)
    value_cube = values.reshape(WINDOW_TOKENS, KEY_VALUE_HEADS, HEAD_SIZE)
    positions = jnp.arange(WINDOW_TOKENS, dtype=jnp.int32)
    outputs = []
    for query_range in range(N_KEY):
        first_query = query_range * TOK_DEV
        query_block = query_three[first_query:first_query + TOK_DEV]
        piece_list = []
        total_list = []
        for offset in range(min(REACH, query_range) + 1):
            first_key = (query_range - offset) * TOK_DEV
            piece, log_total = partial_block(query_block, key_cube[first_key:first_key + TOK_DEV], value_cube[first_key:first_key + TOK_DEV], doc_ids[first_query:first_query + TOK_DEV], doc_ids[first_key:first_key + TOK_DEV], positions[first_query:first_query + TOK_DEV], positions[first_key:first_key + TOK_DEV])
            piece_list.append(piece)
            total_list.append(log_total)
        pieces = jnp.stack(piece_list)
        log_totals = jnp.stack(total_list)
        top = lax.optimization_barrier(jnp.max(log_totals, axis=0))
        factors = jnp.exp(log_totals - top[None])
        numerator = lax.optimization_barrier(jnp.sum(factors[..., None] * pieces.astype(jnp.float32), axis=0))
        denominator = lax.optimization_barrier(jnp.sum(factors, axis=0))
        outputs.append((numerator / denominator[..., None]).astype(jnp.bfloat16))
    attn = jnp.concatenate(outputs, axis=0).reshape(WINDOW_TOKENS, QUERY_HEADS * HEAD_SIZE)
    return jnp.dot(attn, out_weight, preferred_element_type=jnp.float32).astype(jnp.bfloat16)
```

```python
import functools
import math

import jax
import jax.numpy as jnp
from jax import lax
from jax.experimental import pallas as pl
from jax.experimental.pallas import tpu as pltpu
from jax.sharding import PartitionSpec as P

QUERY_HEADS = 64
KEY_VALUE_HEADS = 8
HEAD_SIZE = 128

very_low = -1e30
MESH = pl.DeviceIdType.MESH


def kernel(dims, doc_ref, q_hbm, k_hbm, v_hbm, w_hbm, out_ref,
           qs, kvbuf, wv, acc, mx, gath, psend, rbuf, own,
           load_sem, w_sem, zs, zr, gs, gr, ys, yr):
    n_key, n_tok, n_kv, reach, heads, rows, ch, sub, n_col, ct = dims
    xs = n_tok // 2
    block = ch * sub
    n_ch = n_kv * sub
    group = QUERY_HEADS // KEY_VALUE_HEADS
    key = lax.axis_index("key")
    tok = lax.axis_index("tok")
    kv = lax.axis_index("kv")
    tx, core = tok // 2, tok % 2
    mate = tx * 2 + (1 - core)
    kv_local = (tok * heads) // group
    has_next = key + 1 < n_key

    barrier = pltpu.get_barrier_semaphore()

    def greet(where):
        pl.semaphore_signal(barrier, inc=1, device_id=where, device_id_type=MESH)

    @pl.when(key > 0)
    def _():
        greet({"key": key - 1})

    @pl.when(has_next)
    def _():
        greet({"key": key + 1})

    greet({"tok": mate})
    for d in range(1, xs):
        greet({"tok": ((tx + d) % xs) * 2 + core})
    for d in range(1, n_kv):
        greet({"kv": (kv + d) % n_kv})

    cols = pl.ds(pl.multiple_of(kv_local * HEAD_SIZE, HEAD_SIZE), HEAD_SIZE)
    kload = pltpu.make_async_copy(k_hbm.at[:, cols], kvbuf.at[0, 0], load_sem.at[0])
    vload = pltpu.make_async_copy(v_hbm.at[:, cols], kvbuf.at[0, 1], load_sem.at[1])
    kload.start()
    vload.start()
    qloads = []
    for h in range(heads):
        cp = pltpu.make_async_copy(
            q_hbm.at[:, h * HEAD_SIZE:(h + 1) * HEAD_SIZE], qs.at[h], load_sem.at[2 + h])
        cp.start()
        qloads.append(cp)
    wloads = []
    for n in range(n_col):
        cp = pltpu.make_async_copy(w_hbm.at[:, n * ct:(n + 1) * ct], wv.at[n], w_sem.at[n])
        cp.start()
        wloads.append(cp)
    kload.wait()
    vload.wait()
    greeted = 1 + (xs - 1) + (n_kv - 1)
    pl.semaphore_wait(
        barrier,
        greeted + jnp.where(key > 0, 1, 0) + jnp.where(has_next, 1, 0))

    def zcopy(slot):
        return pltpu.make_async_remote_copy(
            src_ref=kvbuf.at[slot], dst_ref=kvbuf.at[slot + 1],
            send_sem=zs.at[slot], recv_sem=zr.at[slot],
            device_id={"key": key + 1}, device_id_type=MESH)

    @pl.when(has_next)
    def _():
        zcopy(0).start()

    for cp in qloads:
        cp.wait()

    factor = math.log2(math.e) / math.sqrt(HEAD_SIZE)

    def update(r, slot):
        start = pl.multiple_of(r * ch, ch)
        q = qs[:, pl.ds(start, ch), :].reshape(heads * ch, HEAD_SIZE)
        k = kvbuf[slot, 0]
        v = kvbuf[slot, 1]
        s = lax.dot_general(q, k, (((1,), (1,)), ((), ())), preferred_element_type=jnp.float32)
        kdoc = doc_ref[pl.ds(key - slot, 1), :]
        qdoc = doc_ref[pl.ds(key, 1), :]
        at = lax.broadcasted_iota(jnp.int32, (ch, rows), 1)
        row = lax.broadcasted_iota(jnp.int32, (ch, rows), 0) + start
        qcol = jnp.sum(jnp.where(at == row, qdoc, 0), axis=1, keepdims=True)
        allowed = qcol == kdoc
        if slot == 0:
            allowed = allowed & (at <= row)
        bias = jnp.where(allowed, 0.0, very_low)
        s = s.reshape(heads, ch, rows) + bias[None]
        m = jnp.max(s, axis=2, keepdims=True)
        if slot > 0:
            old = mx[r].reshape(heads, ch, HEAD_SIZE)
            m = jnp.maximum(m, old[:, :, :1])
        p = jnp.exp2((s - m) * factor).astype(jnp.bfloat16).reshape(heads * ch, rows)
        ve = jnp.concatenate([v, jnp.ones_like(v)], axis=1)
        pv = jnp.dot(p, ve, preferred_element_type=jnp.float32)
        wide = jnp.broadcast_to(m, (heads, ch, HEAD_SIZE))
        if slot > 0:
            fade = jnp.exp2((old - wide) * factor).reshape(heads * ch, HEAD_SIZE)
            pv = pv + acc[r] * jnp.concatenate([fade, fade], axis=1)
        mx[r] = wide.reshape(heads * ch, HEAD_SIZE)
        acc[r] = pv

    for slot in range(reach):
        @pl.when(key >= slot)
        def _(slot=slot):
            if slot > 0:
                zcopy(slot - 1).wait_recv()

                @pl.when(has_next)
                def _():
                    zcopy(slot).start()
            lax.fori_loop(0, n_ch, lambda r, x: (update(r, slot), x)[1], 0)

    @pl.when(key >= reach)
    def _():
        zcopy(reach - 1).wait_recv()

    def gcopy(c, who, where, sem):
        return pltpu.make_async_remote_copy(
            src_ref=gath.at[c, who], dst_ref=gath.at[c, who],
            send_sem=gs.at[c, sem], recv_sem=gr.at[c, who],
            device_id={"tok": where}, device_id_type=MESH)

    def to_x(c, d):
        return gcopy(c, tok, ((tx + d) % xs) * 2 + core, d - 1)

    def from_x(c, d):
        who = ((tx + d) % xs) * 2 + core
        return gcopy(c, who, who, 0)

    def finish(c):
        r = ((kv + 1 + c // sub) % n_kv) * sub + c % sub

        @pl.when(key >= reach)
        def _():
            update(r, reach)

        a = acc[r]
        o = a[:, :HEAD_SIZE] / a[:, HEAD_SIZE:]
        gath[c, tok] = o.astype(jnp.bfloat16).reshape(heads, ch, HEAD_SIZE)
        for d in range(1, xs):
            to_x(c, d).start()
        gcopy(c, tok, mate, xs - 1).start()

    def forward(c):
        for d in range(1, xs):
            from_x(c, d).wait_recv()
            who = ((tx + d) % xs) * 2 + core
            gcopy(c, who, mate, xs - 1 + d).start()

    def ycopy(c, n):
        d = c // sub + 1
        return pltpu.make_async_remote_copy(
            src_ref=psend.at[c, n], dst_ref=rbuf.at[c, n],
            send_sem=ys.at[c, n], recv_sem=yr.at[c, n],
            device_id={"kv": (kv + d) % n_kv}, device_id_type=MESH)

    n_send = n_ch - sub

    def multiply(c):
        for x in range(xs):
            gcopy(c, x * 2 + (1 - core), mate, 0).wait_recv()
        pieces = [gath[c, t, h] for t in range(n_tok) for h in range(heads)]
        lhs = jnp.concatenate(pieces, axis=1)

        def column(n, x):
            part = jnp.dot(lhs, wv[n], preferred_element_type=jnp.float32)
            if c < n_send:
                psend[c, n] = part.astype(jnp.bfloat16)
                ycopy(c, n).start()
            else:
                own[c - n_send, n] = part
            return x

        lax.fori_loop(0, n_col, column, 0)

    lead = min(2, n_ch - 1)
    for c in range(lead + 1):
        finish(c)
    forward(0)
    for c in range(lead + 1, n_ch):
        finish(c)
    for cp in wloads:
        cp.wait()
    for c in range(n_ch):
        if c + 1 < n_ch and c > 0:
            forward(c + 1)
        multiply(c)
        if c == 0 and n_ch > 1:
            forward(1)

    for s in range(sub):
        for n in range(n_col):
            total = own[s, n]
            for d in range(1, n_kv):
                c = (d - 1) * sub + s
                ycopy(c, n).wait_recv()
                total = total + rbuf[c, n].astype(jnp.float32)
            out_ref[s * ch:(s + 1) * ch, n * ct:(n + 1) * ct] = total.astype(jnp.bfloat16)

    for slot in range(reach):
        @pl.when((key >= slot) & has_next)
        def _(slot=slot):
            zcopy(slot).wait_send()
    for c in range(n_ch):
        for i in range(2 * xs - 1):
            gcopy(c, tok, mate, i).wait_send()
        if c < n_send:
            for n in range(n_col):
                ycopy(c, n).wait_send()


def per_device(sizes, queries, keys, values, doc_ids, out_weight):
    n_kv, n_key, n_tok = sizes
    rows, width = queries.shape
    heads = width // HEAD_SIZE
    depth, features = out_weight.shape
    reach = n_key // 2
    block = rows // n_kv
    sub = 2 if block >= 128 else 1
    ch = block // sub
    n_ch = n_kv * sub
    ct = min(512, features)
    n_col = features // ct
    n_send = n_ch - sub
    dims = (n_key, n_tok, n_kv, reach, heads, rows, ch, sub, n_col, ct)
    bf, f32 = jnp.bfloat16, jnp.float32
    hbm = pl.BlockSpec(memory_space=pl.ANY)
    vmem = pl.BlockSpec(memory_space=pltpu.VMEM)
    dma = pltpu.SemaphoreType.DMA
    flops = 2 * rows * depth * features + 4 * rows * rows * width * (reach + 1)
    return pl.pallas_call(
        functools.partial(kernel, dims),
        out_shape=jax.ShapeDtypeStruct((block, features), bf),
        in_specs=[vmem, hbm, hbm, hbm, hbm],
        out_specs=vmem,
        scratch_shapes=[
            pltpu.VMEM((heads, rows, HEAD_SIZE), bf),
            pltpu.VMEM((reach + 1, 2, rows, HEAD_SIZE), bf),
            pltpu.VMEM((n_col, depth, ct), bf),
            pltpu.VMEM((n_ch, heads * ch, 2 * HEAD_SIZE), f32),
            pltpu.VMEM((n_ch, heads * ch, HEAD_SIZE), f32),
            pltpu.VMEM((n_ch, n_tok, heads, ch, HEAD_SIZE), bf),
            pltpu.VMEM((n_send, n_col, ch, ct), bf),
            pltpu.VMEM((n_send, n_col, ch, ct), bf),
            pltpu.VMEM((sub, n_col, ch, ct), f32),
            dma((2 + heads,)),
            dma((n_col,)),
            dma((reach,)),
            dma((reach,)),
            dma((n_ch, n_tok)),
            dma((n_ch, n_tok)),
            dma((n_send, n_col)),
            dma((n_send, n_col)),
        ],
        compiler_params=pltpu.CompilerParams(
            collective_id=0, has_side_effects=True, vmem_limit_bytes=48 * 1024 * 1024),
        cost_estimate=pl.CostEstimate(
            flops=flops, bytes_accessed=2 * depth * features, transcendentals=0),
    )(doc_ids.reshape(n_key, rows), queries, keys, values, out_weight)


def solution(mesh):
    sizes = tuple(mesh.shape[a] for a in ("kv", "key", "tok"))
    placed = (P("key", ("kv", "tok")), P("key", "kv"), P("key", "kv"), P(), P("kv", "tok"))
    return jax.shard_map(
        functools.partial(per_device, sizes), mesh=mesh, in_specs=placed,
        out_specs=P(("key", "kv"), "tok"), check_vma=False
    )
```

```python
import functools
import math

import jax
import jax.numpy as jnp
from jax import lax
from jax.experimental import pallas as pl
from jax.experimental.pallas import tpu as pltpu
from jax.sharding import PartitionSpec as P

QUERY_HEADS = 64
KEY_VALUE_HEADS = 8
HEAD_SIZE = 128

very_low = -1e30
MESH = pl.DeviceIdType.MESH


def kernel(dims, doc_ref, q_hbm, k_hbm, v_hbm, w_hbm, out_ref,
           qs, kvbuf, wv, acc, mx, gath, psend, rbuf, own,
           load_sem, w_sem, zs, zr, gs, gr, ys, yr):
    n_key, n_tok, n_kv, reach, heads, rows, ch, sub, n_col, ct = dims
    xs = n_tok // 2
    block = ch * sub
    n_ch = n_kv * sub
    group = QUERY_HEADS // KEY_VALUE_HEADS
    key = lax.axis_index("key")
    tok = lax.axis_index("tok")
    kv = lax.axis_index("kv")
    tx, core = tok // 2, tok % 2
    mate = tx * 2 + (1 - core)
    kv_local = (tok * heads) // group
    has_next = key + 1 < n_key

    barrier = pltpu.get_barrier_semaphore()

    def greet(where):
        pl.semaphore_signal(barrier, inc=1, device_id=where, device_id_type=MESH)

    @pl.when(key > 0)
    def _():
        greet({"key": key - 1})

    @pl.when(has_next)
    def _():
        greet({"key": key + 1})

    greet({"tok": mate})
    for d in range(1, xs):
        greet({"tok": ((tx + d) % xs) * 2 + core})
    for d in range(1, n_kv):
        greet({"kv": (kv + d) % n_kv})

    cols = pl.ds(pl.multiple_of(kv_local * HEAD_SIZE, HEAD_SIZE), HEAD_SIZE)
    kload = pltpu.make_async_copy(k_hbm.at[:, cols], kvbuf.at[0, 0], load_sem.at[0])
    vload = pltpu.make_async_copy(v_hbm.at[:, cols], kvbuf.at[0, 1], load_sem.at[1])
    kload.start()
    vload.start()
    qloads = []
    for h in range(heads):
        cp = pltpu.make_async_copy(
            q_hbm.at[:, h * HEAD_SIZE:(h + 1) * HEAD_SIZE], qs.at[h], load_sem.at[2 + h])
        cp.start()
        qloads.append(cp)
    wloads = []
    for n in range(n_col):
        cp = pltpu.make_async_copy(w_hbm.at[:, n * ct:(n + 1) * ct], wv.at[n], w_sem.at[n])
        cp.start()
        wloads.append(cp)
    kload.wait()
    vload.wait()
    greeted = 1 + (xs - 1) + (n_kv - 1)
    pl.semaphore_wait(
        barrier,
        greeted + jnp.where(key > 0, 1, 0) + jnp.where(has_next, 1, 0))

    def zcopy(slot):
        return pltpu.make_async_remote_copy(
            src_ref=kvbuf.at[slot], dst_ref=kvbuf.at[slot + 1],
            send_sem=zs.at[slot], recv_sem=zr.at[slot],
            device_id={"key": key + 1}, device_id_type=MESH)

    @pl.when(has_next)
    def _():
        zcopy(0).start()

    for cp in qloads:
        cp.wait()

    factor = math.log2(math.e) / math.sqrt(HEAD_SIZE)

    def update(r, slot):
        start = pl.multiple_of(r * ch, ch)
        q = qs[:, pl.ds(start, ch), :].reshape(heads * ch, HEAD_SIZE)
        k = kvbuf[slot, 0]
        v = kvbuf[slot, 1]
        s = lax.dot_general(q, k, (((1,), (1,)), ((), ())), preferred_element_type=jnp.float32)
        kdoc = doc_ref[pl.ds(key - slot, 1), :]
        qdoc = doc_ref[pl.ds(key, 1), :]
        at = lax.broadcasted_iota(jnp.int32, (ch, rows), 1)
        row = lax.broadcasted_iota(jnp.int32, (ch, rows), 0) + start
        qcol = jnp.sum(jnp.where(at == row, qdoc, 0), axis=1, keepdims=True)
        allowed = qcol == kdoc
        if slot == 0:
            allowed = allowed & (at <= row)
        bias = jnp.where(allowed, 0.0, very_low)
        s = s.reshape(heads, ch, rows) + bias[None]
        m = jnp.max(s, axis=2, keepdims=True)
        if slot > 0:
            old = mx[r].reshape(heads, ch, HEAD_SIZE)
            m = jnp.maximum(m, old[:, :, :1])
        p = jnp.exp2((s - m) * factor).astype(jnp.bfloat16).reshape(heads * ch, rows)
        ve = jnp.concatenate([v, jnp.ones_like(v)], axis=1)
        pv = jnp.dot(p, ve, preferred_element_type=jnp.float32)
        wide = jnp.broadcast_to(m, (heads, ch, HEAD_SIZE))
        if slot > 0:
            fade = jnp.exp2((old - wide) * factor).reshape(heads * ch, HEAD_SIZE)
            pv = pv + acc[r] * jnp.concatenate([fade, fade], axis=1)
        mx[r] = wide.reshape(heads * ch, HEAD_SIZE)
        acc[r] = pv

    for slot in range(reach):
        @pl.when(key >= slot)
        def _(slot=slot):
            if slot > 0:
                zcopy(slot - 1).wait_recv()

                @pl.when(has_next)
                def _():
                    zcopy(slot).start()
            lax.fori_loop(0, n_ch, lambda r, x: (update(r, slot), x)[1], 0)

    @pl.when(key >= reach)
    def _():
        zcopy(reach - 1).wait_recv()

    def gcopy(c, who, where, sem):
        return pltpu.make_async_remote_copy(
            src_ref=gath.at[c, who], dst_ref=gath.at[c, who],
            send_sem=gs.at[c, sem], recv_sem=gr.at[c, who],
            device_id={"tok": where}, device_id_type=MESH)

    def to_x(c, d):
        return gcopy(c, tok, ((tx + d) % xs) * 2 + core, d - 1)

    def from_x(c, d):
        who = ((tx + d) % xs) * 2 + core
        return gcopy(c, who, who, 0)

    def finish(c):
        r = ((kv + 1 + c // sub) % n_kv) * sub + c % sub

        @pl.when(key >= reach)
        def _():
            update(r, reach)

        a = acc[r]
        o = a[:, :HEAD_SIZE] / a[:, HEAD_SIZE:]
        gath[c, tok] = o.astype(jnp.bfloat16).reshape(heads, ch, HEAD_SIZE)
        for d in range(1, xs):
            to_x(c, d).start()
        gcopy(c, tok, mate, xs - 1).start()

    def forward(c):
        for d in range(1, xs):
            from_x(c, d).wait_recv()
            who = ((tx + d) % xs) * 2 + core
            gcopy(c, who, mate, xs - 1 + d).start()

    def ycopy(c, n):
        d = c // sub + 1
        return pltpu.make_async_remote_copy(
            src_ref=psend.at[c, n], dst_ref=rbuf.at[c, n],
            send_sem=ys.at[c, n], recv_sem=yr.at[c, n],
            device_id={"kv": (kv + d) % n_kv}, device_id_type=MESH)

    n_send = n_ch - sub

    width = heads * HEAD_SIZE

    def lhs_of(c, t):
        return jnp.concatenate([gath[c, t, h] for h in range(heads)], axis=1)

    def near():
        for c in range(n_ch):
            gcopy(c, mate, mate, 0).wait_recv()
        lhs = jnp.concatenate(
            [jnp.concatenate([lhs_of(c, tx * 2), lhs_of(c, tx * 2 + 1)], axis=1)
             for c in range(n_ch)], axis=0)

        def column(n, x):
            w = wv[n, pl.ds(pl.multiple_of(tx * 2 * width, width), 2 * width), :]
            part = jnp.dot(lhs, w, preferred_element_type=jnp.float32)
            for c in range(n_ch):
                own[c, n] = part[c * ch:(c + 1) * ch]
            return x

        lax.fori_loop(0, n_col, column, 0)

    def far(c, who, last):
        lhs = lhs_of(c, who)

        def column(n, x):
            w = wv[n, pl.ds(pl.multiple_of(who * width, width), width), :]
            part = own[c, n] + jnp.dot(lhs, w, preferred_element_type=jnp.float32)
            if last and c < n_send:
                psend[c, n] = part.astype(jnp.bfloat16)
                ycopy(c, n).start()
            else:
                own[c, n] = part
            return x

        lax.fori_loop(0, n_col, column, 0)

    for c in range(n_ch):
        finish(c)
    for cp in wloads:
        cp.wait()
    near()
    for c in range(n_ch):
        forward(c)
        for d in range(1, xs):
            far(c, ((tx + d) % xs) * 2 + core, False)
        for d in range(1, xs):
            who = ((tx + d) % xs) * 2 + (1 - core)
            gcopy(c, who, mate, 0).wait_recv()
            far(c, who, d == xs - 1)

    for s in range(sub):
        for n in range(n_col):
            total = own[n_send + s, n]
            for d in range(1, n_kv):
                c = (d - 1) * sub + s
                ycopy(c, n).wait_recv()
                total = total + rbuf[c, n].astype(jnp.float32)
            out_ref[s * ch:(s + 1) * ch, n * ct:(n + 1) * ct] = total.astype(jnp.bfloat16)

    for slot in range(reach):
        @pl.when((key >= slot) & has_next)
        def _(slot=slot):
            zcopy(slot).wait_send()
    for c in range(n_ch):
        for i in range(2 * xs - 1):
            gcopy(c, tok, mate, i).wait_send()
        if c < n_send:
            for n in range(n_col):
                ycopy(c, n).wait_send()


def per_device(sizes, queries, keys, values, doc_ids, out_weight):
    n_kv, n_key, n_tok = sizes
    rows, width = queries.shape
    heads = width // HEAD_SIZE
    depth, features = out_weight.shape
    reach = n_key // 2
    block = rows // n_kv
    sub = 2 if block >= 128 else 1
    ch = block // sub
    n_ch = n_kv * sub
    ct = min(512, features)
    n_col = features // ct
    n_send = n_ch - sub
    dims = (n_key, n_tok, n_kv, reach, heads, rows, ch, sub, n_col, ct)
    bf, f32 = jnp.bfloat16, jnp.float32
    hbm = pl.BlockSpec(memory_space=pl.ANY)
    vmem = pl.BlockSpec(memory_space=pltpu.VMEM)
    dma = pltpu.SemaphoreType.DMA
    flops = 2 * rows * depth * features + 4 * rows * rows * width * (reach + 1)
    return pl.pallas_call(
        functools.partial(kernel, dims),
        out_shape=jax.ShapeDtypeStruct((block, features), bf),
        in_specs=[vmem, hbm, hbm, hbm, hbm],
        out_specs=vmem,
        scratch_shapes=[
            pltpu.VMEM((heads, rows, HEAD_SIZE), bf),
            pltpu.VMEM((reach + 1, 2, rows, HEAD_SIZE), bf),
            pltpu.VMEM((n_col, depth, ct), bf),
            pltpu.VMEM((n_ch, heads * ch, 2 * HEAD_SIZE), f32),
            pltpu.VMEM((n_ch, heads * ch, HEAD_SIZE), f32),
            pltpu.VMEM((n_ch, n_tok, heads, ch, HEAD_SIZE), bf),
            pltpu.VMEM((n_send, n_col, ch, ct), bf),
            pltpu.VMEM((n_send, n_col, ch, ct), bf),
            pltpu.VMEM((n_ch, n_col, ch, ct), f32),
            dma((2 + heads,)),
            dma((n_col,)),
            dma((reach,)),
            dma((reach,)),
            dma((n_ch, n_tok)),
            dma((n_ch, n_tok)),
            dma((n_send, n_col)),
            dma((n_send, n_col)),
        ],
        compiler_params=pltpu.CompilerParams(
            collective_id=0, has_side_effects=True, vmem_limit_bytes=48 * 1024 * 1024),
        cost_estimate=pl.CostEstimate(
            flops=flops, bytes_accessed=2 * depth * features, transcendentals=0),
    )(doc_ids.reshape(n_key, rows), queries, keys, values, out_weight)


def solution(mesh):
    sizes = tuple(mesh.shape[a] for a in ("kv", "key", "tok"))
    placed = (P("key", ("kv", "tok")), P("key", "kv"), P("key", "kv"), P(), P("kv", "tok"))
    return jax.shard_map(
        functools.partial(per_device, sizes), mesh=mesh, in_specs=placed,
        out_specs=P(("key", "kv"), "tok"), check_vma=False
    )
```

```python
import functools
import math

import jax
import jax.numpy as jnp
from jax import lax
from jax.experimental import pallas as pl
from jax.experimental.pallas import tpu as pltpu
from jax.sharding import PartitionSpec as P

QUERY_HEADS = 64
KEY_VALUE_HEADS = 8
HEAD_SIZE = 128

very_low = -1e30
MESH = pl.DeviceIdType.MESH


def kernel(dims, doc_ref, q_hbm, k_hbm, v_hbm, w_hbm, out_ref,
           qs, kvbuf, wv, acc, mx, gath, psend, rbuf, own,
           load_sem, w_sem, zs, zr, gs, gr, ys, yr):
    n_key, n_tok, n_kv, reach, heads, rows, ch, sub, n_col, ct = dims
    xs = n_tok // 2
    block = ch * sub
    n_ch = n_kv * sub
    group = QUERY_HEADS // KEY_VALUE_HEADS
    key = lax.axis_index("key")
    tok = lax.axis_index("tok")
    kv = lax.axis_index("kv")
    tx, core = tok // 2, tok % 2
    mate = tx * 2 + (1 - core)
    kv_local = (tok * heads) // group
    has_next = key + 1 < n_key

    barrier = pltpu.get_barrier_semaphore()

    def greet(where):
        pl.semaphore_signal(barrier, inc=1, device_id=where, device_id_type=MESH)

    @pl.when(key > 0)
    def _():
        greet({"key": key - 1})

    @pl.when(has_next)
    def _():
        greet({"key": key + 1})

    greet({"tok": mate})
    for d in range(1, xs):
        greet({"tok": ((tx + d) % xs) * 2 + core})
    for d in range(1, n_kv):
        greet({"kv": (kv + d) % n_kv})

    cols = pl.ds(pl.multiple_of(kv_local * HEAD_SIZE, HEAD_SIZE), HEAD_SIZE)
    kload = pltpu.make_async_copy(k_hbm.at[:, cols], kvbuf.at[0, 0], load_sem.at[0])
    vload = pltpu.make_async_copy(v_hbm.at[:, cols], kvbuf.at[0, 1], load_sem.at[1])
    kload.start()
    vload.start()
    qloads = []
    for h in range(heads):
        cp = pltpu.make_async_copy(
            q_hbm.at[:, h * HEAD_SIZE:(h + 1) * HEAD_SIZE], qs.at[h], load_sem.at[2 + h])
        cp.start()
        qloads.append(cp)
    wloads = []
    for n in range(n_col):
        cp = pltpu.make_async_copy(w_hbm.at[:, n * ct:(n + 1) * ct], wv.at[n], w_sem.at[n])
        cp.start()
        wloads.append(cp)
    kload.wait()
    vload.wait()
    greeted = 1 + (xs - 1) + (n_kv - 1)
    pl.semaphore_wait(
        barrier,
        greeted + jnp.where(key > 0, 1, 0) + jnp.where(has_next, 1, 0))

    def zcopy(slot):
        return pltpu.make_async_remote_copy(
            src_ref=kvbuf.at[slot], dst_ref=kvbuf.at[slot + 1],
            send_sem=zs.at[slot], recv_sem=zr.at[slot],
            device_id={"key": key + 1}, device_id_type=MESH)

    @pl.when(has_next)
    def _():
        zcopy(0).start()

    for cp in qloads:
        cp.wait()

    factor = math.log2(math.e) / math.sqrt(HEAD_SIZE)

    def update(r, slot):
        start = pl.multiple_of(r * ch, ch)
        q = qs[:, pl.ds(start, ch), :].reshape(heads * ch, HEAD_SIZE)
        k = kvbuf[slot, 0]
        v = kvbuf[slot, 1]
        s = lax.dot_general(q, k, (((1,), (1,)), ((), ())), preferred_element_type=jnp.float32)
        kdoc = doc_ref[pl.ds(key - slot, 1), :]
        qdoc = doc_ref[pl.ds(key, 1), :]
        at = lax.broadcasted_iota(jnp.int32, (ch, rows), 1)
        row = lax.broadcasted_iota(jnp.int32, (ch, rows), 0) + start
        qcol = jnp.sum(jnp.where(at == row, qdoc, 0), axis=1, keepdims=True)
        allowed = qcol == kdoc
        if slot == 0:
            allowed = allowed & (at <= row)
        bias = jnp.where(allowed, 0.0, very_low)
        s = s.reshape(heads, ch, rows) + bias[None]
        m = jnp.max(s, axis=2, keepdims=True)
        if slot > 0:
            old = mx[r].reshape(heads, ch, HEAD_SIZE)
            m = jnp.maximum(m, old[:, :, :1])
        p = jnp.exp2((s - m) * factor).astype(jnp.bfloat16).reshape(heads * ch, rows)
        ve = jnp.concatenate([v, jnp.ones_like(v)], axis=1)
        pv = jnp.dot(p, ve, preferred_element_type=jnp.float32)
        wide = jnp.broadcast_to(m, (heads, ch, HEAD_SIZE))
        if slot > 0:
            fade = jnp.exp2((old - wide) * factor).reshape(heads * ch, HEAD_SIZE)
            pv = pv + acc[r] * jnp.concatenate([fade, fade], axis=1)
        mx[r] = wide.reshape(heads * ch, HEAD_SIZE)
        acc[r] = pv

    for slot in range(reach):
        @pl.when(key >= slot)
        def _(slot=slot):
            if slot > 0:
                zcopy(slot - 1).wait_recv()

                @pl.when(has_next)
                def _():
                    zcopy(slot).start()
            lax.fori_loop(0, n_ch, lambda r, x: (update(r, slot), x)[1], 0)

    @pl.when(key >= reach)
    def _():
        zcopy(reach - 1).wait_recv()

    def gcopy(c, who, where, sem):
        return pltpu.make_async_remote_copy(
            src_ref=gath.at[c, who], dst_ref=gath.at[c, who],
            send_sem=gs.at[c, sem], recv_sem=gr.at[c, who],
            device_id={"tok": where}, device_id_type=MESH)

    def to_x(c, d):
        return gcopy(c, tok, ((tx + d) % xs) * 2 + core, d - 1)

    def from_x(c, d):
        who = ((tx + d) % xs) * 2 + core
        return gcopy(c, who, who, 0)

    def finish(c):
        r = ((kv + 1 + c // sub) % n_kv) * sub + c % sub

        @pl.when(key >= reach)
        def _():
            update(r, reach)

        a = acc[r]
        o = a[:, :HEAD_SIZE] / a[:, HEAD_SIZE:]
        gath[c, tok] = o.astype(jnp.bfloat16).reshape(heads, ch, HEAD_SIZE)
        for d in range(1, xs):
            to_x(c, d).start()
        gcopy(c, tok, mate, xs - 1).start()

    def forward(c):
        for d in range(1, xs):
            from_x(c, d).wait_recv()
            who = ((tx + d) % xs) * 2 + core
            gcopy(c, who, mate, xs - 1 + d).start()

    def ycopy(c, n):
        d = c // sub + 1
        return pltpu.make_async_remote_copy(
            src_ref=psend.at[c, n], dst_ref=rbuf.at[c, n],
            send_sem=ys.at[c, n], recv_sem=yr.at[c, n],
            device_id={"kv": (kv + d) % n_kv}, device_id_type=MESH)

    n_send = n_ch - sub

    width = heads * HEAD_SIZE

    def lhs_of(c, t):
        return jnp.concatenate([gath[c, t, h] for h in range(heads)], axis=1)

    def near():
        for c in range(n_ch):
            gcopy(c, mate, mate, 0).wait_recv()
        lhs = jnp.concatenate(
            [jnp.concatenate([lhs_of(c, tx * 2), lhs_of(c, tx * 2 + 1)], axis=1)
             for c in range(n_ch)], axis=0)

        def column(n, x):
            w = wv[n, pl.ds(pl.multiple_of(tx * 2 * width, width), 2 * width), :]
            part = jnp.dot(lhs, w, preferred_element_type=jnp.float32)
            for c in range(n_ch):
                own[c, n] = part[c * ch:(c + 1) * ch]
            return x

        lax.fori_loop(0, n_col, column, 0)

    def far(c, who, last):
        lhs = lhs_of(c, who)

        def column(n, x):
            w = wv[n, pl.ds(pl.multiple_of(who * width, width), width), :]
            part = own[c, n] + jnp.dot(lhs, w, preferred_element_type=jnp.float32)
            if last and c < n_send:
                psend[c, n] = part.astype(jnp.bfloat16)
                ycopy(c, n).start()
            else:
                own[c, n] = part
            return x

        lax.fori_loop(0, n_col, column, 0)

    for c in range(n_ch):
        finish(c)
    for cp in wloads:
        cp.wait()
    near()
    forward(0)
    for c in range(n_ch):
        for d in range(1, xs):
            far(c, ((tx + d) % xs) * 2 + core, False)
        if c + 1 < n_ch:
            forward(c + 1)
        for d in range(1, xs):
            who = ((tx + d) % xs) * 2 + (1 - core)
            gcopy(c, who, mate, 0).wait_recv()
            far(c, who, d == xs - 1)

    for s in range(sub):
        for n in range(n_col):
            total = own[n_send + s, n]
            for d in range(1, n_kv):
                c = (d - 1) * sub + s
                ycopy(c, n).wait_recv()
                total = total + rbuf[c, n].astype(jnp.float32)
            out_ref[s * ch:(s + 1) * ch, n * ct:(n + 1) * ct] = total.astype(jnp.bfloat16)

    for slot in range(reach):
        @pl.when((key >= slot) & has_next)
        def _(slot=slot):
            zcopy(slot).wait_send()
    for c in range(n_ch):
        for i in range(2 * xs - 1):
            gcopy(c, tok, mate, i).wait_send()
        if c < n_send:
            for n in range(n_col):
                ycopy(c, n).wait_send()


def per_device(sizes, queries, keys, values, doc_ids, out_weight):
    n_kv, n_key, n_tok = sizes
    rows, width = queries.shape
    heads = width // HEAD_SIZE
    depth, features = out_weight.shape
    reach = n_key // 2
    block = rows // n_kv
    sub = 2 if block >= 128 else 1
    ch = block // sub
    n_ch = n_kv * sub
    ct = min(512, features)
    n_col = features // ct
    n_send = n_ch - sub
    dims = (n_key, n_tok, n_kv, reach, heads, rows, ch, sub, n_col, ct)
    bf, f32 = jnp.bfloat16, jnp.float32
    hbm = pl.BlockSpec(memory_space=pl.ANY)
    vmem = pl.BlockSpec(memory_space=pltpu.VMEM)
    dma = pltpu.SemaphoreType.DMA
    flops = 2 * rows * depth * features + 4 * rows * rows * width * (reach + 1)
    return pl.pallas_call(
        functools.partial(kernel, dims),
        out_shape=jax.ShapeDtypeStruct((block, features), bf),
        in_specs=[vmem, hbm, hbm, hbm, hbm],
        out_specs=vmem,
        scratch_shapes=[
            pltpu.VMEM((heads, rows, HEAD_SIZE), bf),
            pltpu.VMEM((reach + 1, 2, rows, HEAD_SIZE), bf),
            pltpu.VMEM((n_col, depth, ct), bf),
            pltpu.VMEM((n_ch, heads * ch, 2 * HEAD_SIZE), f32),
            pltpu.VMEM((n_ch, heads * ch, HEAD_SIZE), f32),
            pltpu.VMEM((n_ch, n_tok, heads, ch, HEAD_SIZE), bf),
            pltpu.VMEM((n_send, n_col, ch, ct), bf),
            pltpu.VMEM((n_send, n_col, ch, ct), bf),
            pltpu.VMEM((n_ch, n_col, ch, ct), f32),
            dma((2 + heads,)),
            dma((n_col,)),
            dma((reach,)),
            dma((reach,)),
            dma((n_ch, n_tok)),
            dma((n_ch, n_tok)),
            dma((n_send, n_col)),
            dma((n_send, n_col)),
        ],
        compiler_params=pltpu.CompilerParams(
            collective_id=0, has_side_effects=True, vmem_limit_bytes=48 * 1024 * 1024),
        cost_estimate=pl.CostEstimate(
            flops=flops, bytes_accessed=2 * depth * features, transcendentals=0),
    )(doc_ids.reshape(n_key, rows), queries, keys, values, out_weight)


def solution(mesh):
    sizes = tuple(mesh.shape[a] for a in ("kv", "key", "tok"))
    placed = (P("key", ("kv", "tok")), P("key", "kv"), P("key", "kv"), P(), P("kv", "tok"))
    return jax.shard_map(
        functools.partial(per_device, sizes), mesh=mesh, in_specs=placed,
        out_specs=P(("key", "kv"), "tok"), check_vma=False
    )
```
